256 devices in a mesh: blk: 64 (over z, y, x_hi), tp: 4 (over x_lo, core).
Axes of the slice: x: 4 (x_hi: 2, x_lo: 2; x = x_hi * 2 + x_lo), y: 4, z: 8, core: 2. Of those that a mesh axis runs over, the one named last changes fastest.
Arguments:
- stream: bfloat16 [16384, 2560], P('blk', 'tp'), may hold values from -180 to 180, as said below
- norm_gain: bfloat16 [2560], P('tp'), may hold values from 0.099609375 to 1.8984375
- gate_weight: bfloat16 [2560, 7168], P('blk', 'tp'), may hold values from -0.125 to 0.125
- act_grad: bfloat16 [16384, 7168], P('blk', 'tp'), may hold values from -36 to 36
Outputs:
- gate_act: bfloat16 [16384, 7168], P('blk', 'tp')
- input_grad: bfloat16 [16384, 2560], P('blk', 'tp')
- weight_grad: float32 [2560, 7168], P('blk', 'tp')
- gain_grad: float32 [2560], P('tp')
The draws below stay inside these ranges and needn't reach their ends.
Inputs may be any that keep to these rules, and one draw needn't show every extreme that they name: `stream`: token rows and feature columns carry independent scales.
All inputs are finite; a program needn't handle non-finite values.
Results may differ from the reference program's by a relative error of at most 0.015.
Values may be sent and summed in bfloat16 or wider, within the bound.
No kernel may reach another device: no remote copies, remote signals or barrier semaphores. Data moves between devices by JAX's collectives and lax.ppermute only.
A program may use at most 64 MiB of HBM per device.

```python
import math
import jax
import jax.numpy as jnp
from jax import lax

D = 2560
F = 7168
TOKENS = 16384
N_TP = 4


def draw_stream(key, part):
    key = jax.random.fold_in(key, 11)
    key_base, key_rows, key_cols = jax.random.split(key, 3)
    col_rise = 1.0 + 2.0 * jnp.arange(D, dtype=jnp.float32) / D
    col_scale = jnp.exp(jax.random.uniform(key_cols, (1, D)) * math.log(10.0)) * col_rise
    entries = jax.random.truncated_normal(key_base, -4.0, 4.0, (TOKENS, D))
    row_scale = jnp.exp(jax.random.uniform(key_rows, (TOKENS, 1)) * math.log(10.0))
    return (0.15 * entries * row_scale * col_scale).astype(jnp.bfloat16)


def draw_act_grad(key, part):
    key = jax.random.fold_in(key, 23)
    key_base = jax.random.fold_in(key, 0)
    position = jnp.arange(TOKENS, dtype=jnp.float32)[:, None] / TOKENS
    entries = jax.random.truncated_normal(key_base, -4.0, 4.0, (TOKENS, F))
    values = entries * (1.0 + 2.0 * position)
    return values.astype(jnp.bfloat16)


def steps_of(stream_key, dims, cuts, low, largest):
    def one(dim, shards_of):
        steps = jax.random.uniform(jax.random.fold_in(jax.random.fold_in(stream_key, 6), dim), (shards_of,), jnp.float32, low / len(cuts), largest / len(cuts))
        return jnp.repeat(jnp.exp(steps), dims[dim] // shards_of).reshape((-1,) + (1,) * (len(dims) - dim - 1))

    gain = one(*cuts[0])
    for cut in cuts[1:]:
        gain = gain * one(*cut)
    return gain


def centred(key, dims, width, limit, cuts=(), kind=jnp.bfloat16):
    values = width * jax.random.normal(key, dims, jnp.float32)
    if cuts:
        values = values * steps_of(key, dims, cuts, -0.22, 0.18)
    return jnp.clip(values, -limit, limit).astype(kind)


def setup_inputs(seed: int = 0) -> dict:
    streams_of = jax.random.split(jax.random.key(seed), 5)
    return {
        "stream": draw_stream(jax.random.fold_in(streams_of[4], 71), 0),
        "norm_gain": jnp.clip(1.0 + 0.18 * jax.random.normal(streams_of[1], (D,), jnp.float32), 0.099609375, 1.8984375).astype(jnp.bfloat16),
        "gate_weight": centred(streams_of[2], (D, F), D ** -0.5, 0.125, ((0, 64), (1, 4))),
        "act_grad": draw_act_grad(jax.random.fold_in(streams_of[4], 71), 0),
    }


EPS = 1e-05

def reference(stream, norm_gain, gate_weight, act_grad):
    stream_f = stream.astype(jnp.float32)
    gain_f = norm_gain.astype(jnp.float32)
    inv_rms = lax.rsqrt(lax.optimization_barrier(jnp.sum(stream_f * stream_f, axis=1, keepdims=True)) / D + EPS)
    unit_rows = stream_f * inv_rms
    normed = (unit_rows * gain_f).astype(jnp.bfloat16)
    gate_pre = jnp.dot(normed, gate_weight, preferred_element_type=jnp.float32)
    gate_sig = jax.nn.sigmoid(gate_pre)
    gate_act = (gate_pre * gate_sig).astype(jnp.bfloat16)
    gate_grad = (act_grad.astype(jnp.float32) * gate_sig * (1.0 + gate_pre * (1.0 - gate_sig))).astype(jnp.bfloat16)
    grad_scale = float(TOKENS) ** (-0.5)
    weight_grad = lax.dot_general(normed, gate_grad, (((0,), (0,)), ((), ())), preferred_element_type=jnp.float32) * grad_scale
    normed_f = normed.astype(jnp.float32)
    block_width = F // N_TP
    normed_grad = jnp.zeros((TOKENS, D), jnp.float32)
    inner_sum = jnp.zeros((TOKENS, 1), jnp.float32)
    for block in range(N_TP):
        lower = block * block_width
        partial_value = lax.dot_general(gate_grad[:, lower:lower + block_width], gate_weight[:, lower:lower + block_width], (((1,), (1,)), ((), ())), preferred_element_type=jnp.float32)
        inner_part = lax.optimization_barrier(jnp.sum(partial_value * normed_f, axis=1, keepdims=True)) / D
        part_low = lax.optimization_barrier(partial_value.astype(jnp.bfloat16))
        inner_low = lax.optimization_barrier(inner_part.astype(jnp.bfloat16))
        normed_grad = normed_grad + part_low.astype(jnp.float32)
        inner_sum = inner_sum + inner_low.astype(jnp.float32)
    input_grad = (inv_rms * (normed_grad * gain_f - unit_rows * inner_sum)).astype(jnp.bfloat16)
    gain_grad = lax.optimization_barrier(jnp.sum(normed_grad * unit_rows, axis=0)) * grad_scale
    return (gate_act, input_grad, weight_grad, gain_grad)
```

```python
import jax
import jax.numpy as jnp
from jax import lax
from jax.sharding import Mesh, PartitionSpec as P

D = 2560
EPS = 1e-05
AXES = ("z", "y", "xh", "xl", "c")
SIZES = (8, 4, 2, 2, 2)
X = ("xh", "xl")
BF = jnp.bfloat16
F32 = jnp.float32


def shift(a, axis, n, d):
    return lax.ppermute(a, axis, [(i, (i + d) % n) for i in range(n)])


def swap(a, axis):
    return shift(a, axis, 2, 1)


def two(first, mine, other, axis):
    low = jnp.where(first, mine, other)
    high = jnp.where(first, other, mine)
    return jnp.concatenate([low, high], axis=axis)


def body(stream, norm_gain, gate_weight, act_grad):
    z, y, xh, xl, c = (lax.axis_index(a) for a in AXES)
    x = xh * 2 + xl
    tok, feat = stream.shape
    hid = act_grad.shape[1] // 2
    wrows = gate_weight.shape[0]
    first_h, first_c = xh == 0, c == 0

    w_mine = lax.dynamic_slice_in_dim(gate_weight, xh * hid, hid, 1)
    w_send = lax.dynamic_slice_in_dim(gate_weight, (1 - xh) * hid, hid, 1)
    w_got = swap(w_send, "xh")
    w_block = two(first_h, w_mine, w_got, 0)
    parts = [w_block] + [shift(w_block, "y", 4, -d) for d in (1, 2, 3)]
    twice = jnp.concatenate(parts + parts[:3], axis=0)
    w_y = lax.dynamic_slice_in_dim(twice, lax.rem(4 - y, 4) * 2 * wrows, 8 * wrows, 0)
    weight = lax.all_gather(w_y, "z", axis=0, tiled=True)

    payload = jnp.concatenate([stream, jnp.broadcast_to(norm_gain[None], (16, feat))], axis=0)
    got = [payload] + [shift(payload, X, 4, -d) for d in (1, 2, 3)]
    mine = jnp.concatenate([g[None] for g in got], axis=0)
    both = two(first_c, mine[:, :, None], swap(mine, "c")[:, :, None], 2)
    both = jnp.concatenate([both, both[:3]], axis=0)
    both = lax.dynamic_slice_in_dim(both, lax.rem(4 - x, 4), 4, 0)
    both = both.reshape(2, 2, tok + 16, 2 * feat)
    gain_full = both[0, :, tok].reshape(1, D).astype(F32)
    rows = both[:, :, :tok].transpose(0, 2, 1, 3).reshape(2 * tok, D).astype(F32)
    inv_all = lax.rsqrt(jnp.sum(rows * rows, axis=1, keepdims=True) / D + EPS)
    normed = (rows * inv_all * gain_full).astype(BF)

    a_mine = lax.dynamic_slice_in_dim(act_grad, xh * hid, hid, 1)
    a_send = lax.dynamic_slice_in_dim(act_grad, (1 - xh) * hid, hid, 1)
    cot = two(first_h, a_mine, swap(a_send, "xh"), 0)

    gate_pre = jnp.dot(normed, weight, preferred_element_type=F32)
    sig = jax.nn.sigmoid(gate_pre)
    act = (gate_pre * sig).astype(BF)
    grad_f = cot.astype(F32) * sig * (1.0 + gate_pre * (1.0 - sig))
    gate_grad = grad_f.astype(BF)
    inner = jnp.sum(gate_grad.astype(F32) * gate_pre, axis=1) / D

    scale = float(tok * 64) ** (-0.5)
    terms = lax.dot_general(
        normed, gate_grad, (((0,), (0,)), ((), ())), preferred_element_type=F32
    ).astype(BF)
    rs_z = lax.psum_scatter(terms, "z", scatter_dimension=0, tiled=True)
    block = lambda j: lax.dynamic_slice_in_dim(rs_z, lax.rem(y + j, 4) * 2 * wrows, 2 * wrows, 0)
    total = block(0).astype(F32)
    for d in (1, 2, 3):
        total = total + shift(block(d), "y", 4, d).astype(F32)
    keep = lax.dynamic_slice_in_dim(total, xh * wrows, wrows, 0)
    give = lax.dynamic_slice_in_dim(total, (1 - xh) * wrows, wrows, 0).astype(BF)
    weight_grad = two(first_h, keep, swap(give, "xh").astype(F32), 1) * scale

    o_mine = lax.dynamic_slice_in_dim(act, xh * tok, tok, 0)
    o_send = lax.dynamic_slice_in_dim(act, (1 - xh) * tok, tok, 0)
    gate_act = two(first_h, o_mine, swap(o_send, "xh"), 1)

    part = lax.dot_general(
        gate_grad, weight, (((1,), (1,)), ((), ())), preferred_element_type=F32
    ).reshape(2 * tok, 2, 2, feat)
    p_mine = lax.dynamic_index_in_dim(part, c, 2, keepdims=False)
    p_send = lax.dynamic_index_in_dim(part, 1 - c, 2, keepdims=False).astype(BF)
    half = (p_mine + swap(p_send, "c").astype(F32)).reshape(2, tok, 2, feat)

    def piece(d):
        t = lax.rem(x + d, 4)
        return lax.dynamic_slice(half, (t // 2, 0, t % 2, 0), (1, tok, 1, feat)).reshape(tok, feat)

    normed_grad = piece(0)
    for d in (1, 2, 3):
        normed_grad = normed_grad + shift(piece(d).astype(BF), X, 4, d).astype(F32)
    inner = inner + swap(inner, "c")
    ipiece = lambda d: lax.dynamic_slice_in_dim(inner, lax.rem(x + d, 4) // 2 * tok, tok, 0)
    inner_sum = ipiece(0)
    for d in (1, 2, 3):
        inner_sum = inner_sum + shift(ipiece(d), X, 4, d)
    inner_sum = inner_sum[:, None]

    inv_rms = lax.dynamic_slice_in_dim(inv_all, xh * tok, tok, 0)
    unit_rows = stream.astype(F32) * inv_rms
    gain_f = norm_gain.astype(F32)
    input_grad = (inv_rms * (normed_grad * gain_f - unit_rows * inner_sum)).astype(BF)
    gsum = jnp.sum(normed_grad * unit_rows, axis=0)
    for axis, n, bit in (("xh", 2, 1), ("y", 4, 1), ("y", 4, 2), ("z", 8, 1), ("z", 8, 2), ("z", 8, 4)):
        gsum = gsum + lax.ppermute(gsum, axis, [(i, i ^ bit) for i in range(n)])
    return (gate_act, input_grad, weight_grad, gsum * scale)


def solution(mesh):
    inner_mesh = Mesh(mesh.devices.reshape(SIZES), AXES)
    tokens, features = ("z", "y", "xh"), ("xl", "c")
    return jax.shard_map(
        body,
        mesh=inner_mesh,
        in_specs=(P(tokens, features), P(features), P(tokens, features), P(tokens, features)),
        out_specs=(P(tokens, features), P(tokens, features), P(tokens, features), P(features)),
        check_vma=False,
    )
```

```python
import jax
import jax.numpy as jnp
from jax import lax
from jax.experimental import pallas as pl
from jax.experimental.pallas import tpu as pltpu
from jax.sharding import Mesh, PartitionSpec as P

D = 2560
EPS = 1e-05
AXES = ("z", "y", "xh", "xl", "c")
SIZES = (8, 4, 2, 2, 2)
NUM = dict(zip(AXES, SIZES))
X = ("xh", "xl")
QUAD = ("y", "xh")
BF = jnp.bfloat16
F32 = jnp.float32
VMEM_LIMIT = 40 * 1024 * 1024
NT = (((1,), (1,)), ((), ()))
TN = (((0,), (0,)), ((), ()))


def flip(a, axis, bit):
    names = axis if isinstance(axis, tuple) else (axis,)
    n = 1
    for name in names:
        n *= NUM[name]
    return lax.ppermute(a, axis, [(i, i ^ bit) for i in range(n)])


def ordered(pieces, index):
    low, high = (index % 2) == 0, (index // 2) == 0
    p = pieces
    p = [jnp.where(low, p[0], p[1]), jnp.where(low, p[1], p[0]), jnp.where(low, p[2], p[3]), jnp.where(low, p[3], p[2])]
    return [jnp.where(high, p[0], p[2]), jnp.where(high, p[1], p[3]), jnp.where(high, p[2], p[0]), jnp.where(high, p[3], p[1])]


def norm_kernel(place, mine, other, *refs):
    normed, inv_ref, gain_ref = refs[-3:]
    xl, c = place[0], place[1]
    tok = normed.shape[0]
    feat = mine.shape[-1]
    total = jnp.zeros((tok, 1), F32)
    for src in (mine, other):
        for dxl in (0, 1):
            v = src[0, dxl, :tok, :].astype(F32)
            total = total + jnp.sum(v * v, axis=1, keepdims=True)
    inv = lax.rsqrt(total / D + EPS)
    inv_ref[...] = inv
    for dc, src in enumerate((mine, other)):
        for dxl in (0, 1):
            at = pl.multiple_of(((xl ^ dxl) * 2 + (c ^ dc)) * feat, 128)
            gain = src[0, dxl, tok:, :].astype(F32)[:1]
            v = src[0, dxl, :tok, :].astype(F32)
            normed[:, pl.ds(at, feat)] = (v * inv * gain).astype(BF)
            gain_ref[:, pl.ds(at, feat)] = gain


def norm_call(place, mine, other, half, into):
    _, _, rows, feat = mine.shape
    tok = rows - 16
    block = pl.BlockSpec((1, 2, rows, feat), lambda i, s: (i, 0, 0, 0))
    ins = [mine, other]
    in_specs = [block, block]
    aliases = {}
    if into is not None:
        ins += list(into)
        in_specs += [pl.BlockSpec(memory_space=pl.ANY)] * 3
        aliases = {3: 0, 4: 1, 5: 2}
    return pl.pallas_call(
        norm_kernel,
        out_shape=(
            jax.ShapeDtypeStruct((4 * tok, D), BF),
            jax.ShapeDtypeStruct((4 * tok, 1), F32),
            jax.ShapeDtypeStruct((1, D), F32),
        ),
        grid_spec=pltpu.PrefetchScalarGridSpec(
            num_scalar_prefetch=1,
            grid=(2,),
            in_specs=in_specs,
            out_specs=(
                pl.BlockSpec((tok, D), lambda i, s: (2 * half + i, 0)),
                pl.BlockSpec((tok, 1), lambda i, s: (2 * half + i, 0)),
                pl.BlockSpec((1, D), lambda i, s: (0, 0)),
            ),
        ),
        input_output_aliases=aliases,
        compiler_params=pltpu.CompilerParams(vmem_limit_bytes=VMEM_LIMIT),
        cost_estimate=pl.CostEstimate(flops=8 * tok * D, bytes_accessed=8 * tok * D, transcendentals=0),
        name="norm",
    )(place, *ins)


def gate_kernel(normed, weight, cot, act_ref, grad_ref, inner_ref):
    pre = jnp.dot(normed[...], weight[...], preferred_element_type=F32)
    sig = 1.0 / (1.0 + jnp.exp(-pre))
    act_ref[0] = (pre * sig).astype(BF)
    grad = (cot[0].astype(F32) * sig * (1.0 + pre * (1.0 - sig))).astype(BF)
    grad_ref[...] = grad
    inner_ref[...] = jnp.sum(grad.astype(F32) * pre, axis=1, keepdims=True) / D


def gate_call(normed, weight, cot):
    n, tok, hid = cot.shape
    return pl.pallas_call(
        gate_kernel,
        out_shape=(
            jax.ShapeDtypeStruct((n, tok, hid), BF),
            jax.ShapeDtypeStruct((n * tok, hid), BF),
            jax.ShapeDtypeStruct((n * tok, 1), F32),
        ),
        grid=(n,),
        in_specs=[
            pl.BlockSpec((tok, D), lambda i: (i, 0)),
            pl.BlockSpec((D, hid), lambda i: (0, 0)),
            pl.BlockSpec((1, tok, hid), lambda i: (i, 0, 0)),
        ],
        out_specs=(
            pl.BlockSpec((1, tok, hid), lambda i: (i, 0, 0)),
            pl.BlockSpec((tok, hid), lambda i: (i, 0)),
            pl.BlockSpec((tok, 1), lambda i: (i, 0)),
        ),
        compiler_params=pltpu.CompilerParams(vmem_limit_bytes=VMEM_LIMIT),
        cost_estimate=pl.CostEstimate(
            flops=2 * n * tok * D * hid, bytes_accessed=2 * D * (n * tok + hid), transcendentals=n * tok * hid
        ),
        name="gate",
    )(normed, weight, cot)


def back_kernel(place, grad, weight, normed, inner, gain, own_ref, send_ref, sum_ref):
    xl, c = place[0], place[1]
    feat = own_ref.shape[1] // 2
    first = pl.program_id(0) == 0

    for dc, out in ((1, send_ref), (0, own_ref)):
        for dxl in (0, 1):
            at = pl.multiple_of(((xl ^ dxl) * 2 + (c ^ dc)) * feat, 128)
            part = lax.dot_general(grad[...], weight[pl.ds(at, feat), :], NT, preferred_element_type=F32)
            rows = normed[:, pl.ds(at, feat)].astype(F32)
            g = gain[:, pl.ds(at, feat)]
            out[:, dxl * feat:(dxl + 1) * feat] = (part * g - rows * inner[...] * (1.0 / g)).astype(BF)
            terms = jnp.sum(part * rows, axis=0, keepdims=True)
            old = jnp.where(first, 0.0, sum_ref[:, pl.ds(at, feat)])
            sum_ref[:, pl.ds(at, feat)] = old + terms


def back_call(place, grad, weight, normed, inner, gain, n):
    rows, hid = grad.shape
    tok = rows // n
    return pl.pallas_call(
        back_kernel,
        out_shape=(
            jax.ShapeDtypeStruct((rows, D // 2), BF),
            jax.ShapeDtypeStruct((rows, D // 2), BF),
            jax.ShapeDtypeStruct((1, D), F32),
        ),
        grid_spec=pltpu.PrefetchScalarGridSpec(
            num_scalar_prefetch=1,
            grid=(n,),
            in_specs=[
                pl.BlockSpec((tok, hid), lambda i, s: (i, 0)),
                pl.BlockSpec((D, hid), lambda i, s: (0, 0)),
                pl.BlockSpec((tok, D), lambda i, s: (i, 0)),
                pl.BlockSpec((tok, 1), lambda i, s: (i, 0)),
                pl.BlockSpec((1, D), lambda i, s: (0, 0)),
            ],
            out_specs=(
                pl.BlockSpec((tok, D // 2), lambda i, s: (i, 0)),
                pl.BlockSpec((tok, D // 2), lambda i, s: (i, 0)),
                pl.BlockSpec((1, D), lambda i, s: (0, 0)),
            ),
        ),
        compiler_params=pltpu.CompilerParams(vmem_limit_bytes=VMEM_LIMIT),
        cost_estimate=pl.CostEstimate(
            flops=2 * rows * D * hid, bytes_accessed=2 * D * (2 * rows + hid), transcendentals=0
        ),
        name="back",
    )(place, grad, weight, normed, inner, gain)


def body(stream, norm_gain, gate_weight, act_grad):
    z, y, xh, xl, c = (lax.axis_index(a) for a in AXES)
    yl, yh = lax.rem(y, 2), y // 2
    q = yl * 2 + xh
    tok, feat = stream.shape
    hid = act_grad.shape[1] // 4
    wrows = gate_weight.shape[0]
    place = jnp.stack([xl, c]).astype(jnp.int32)
    scale = float(tok * 64) ** (-0.5)

    cut = lambda a, k: lax.dynamic_slice_in_dim(a, (q ^ k) * hid, hid, 1)
    w_got = [cut(gate_weight, 0)] + [flip(cut(gate_weight, k), QUAD, k) for k in (1, 2, 3)]
    w_quad = jnp.concatenate(ordered(w_got, q), axis=0)
    w_far = flip(w_quad, "y", 2)
    w_y = jnp.concatenate([jnp.where(yh == 0, w_quad, w_far), jnp.where(yh == 0, w_far, w_quad)], axis=0)
    weight = lax.all_gather(w_y, "z", axis=0, tiled=True)

    payload = jnp.concatenate([stream, jnp.broadcast_to(norm_gain[None], (16, feat))], axis=0)
    near = jnp.stack([payload] + [flip(payload, X, m) for m in (1, 2, 3)])
    near = near.reshape(2, 2, tok + 16, feat)
    far = flip(near, "y", 1)
    normed = norm_call(place, near, flip(near, "c", 1), 0, None)
    normed, inv_all, gain = norm_call(place, far, flip(far, "c", 1), 1, normed)

    cot = jnp.stack([cut(act_grad, 0)] + [flip(cut(act_grad, k), QUAD, k) for k in (1, 2, 3)])

    act, gate_grad, inner = gate_call(normed, weight, cot)

    terms = lax.dot_general(normed, gate_grad, TN, preferred_element_type=F32).astype(BF)
    mine = lax.psum_scatter(terms, "z", scatter_dimension=0, tiled=True)
    half = 4 * wrows
    keep = lax.dynamic_slice_in_dim(mine, yh * half, half, 0)
    give = lax.dynamic_slice_in_dim(mine, (1 - yh) * half, half, 0)
    mine = keep.astype(F32) + flip(give, "y", 2).astype(F32)
    rows_of = lambda k: lax.dynamic_slice_in_dim(mine, (q ^ k) * wrows, wrows, 0)
    wg = [rows_of(0)] + [flip(rows_of(k).astype(BF), QUAD, k).astype(F32) for k in (1, 2, 3)]
    weight_grad = jnp.concatenate(ordered(wg, q), axis=1) * scale

    out = [act[0]] + [flip(act[k], QUAD, k) for k in (1, 2, 3)]
    gate_act = jnp.concatenate(ordered(out, q), axis=1)

    own, send, gsum = back_call(place, gate_grad, weight, normed, inner, gain, 4)
    got = flip(send, "c", 1)
    n2 = 2 * tok
    send = (own[n2:].astype(F32) + got[n2:].astype(F32)).astype(BF)
    acc = own[:n2].astype(F32) + got[:n2].astype(F32) + flip(send, "y", 1).astype(F32)
    total = acc[:tok, :feat]
    for m in (1, 2, 3):
        r, f = (m // 2) * tok, (m % 2) * feat
        total = total + flip(acc[r:r + tok, f:f + feat].astype(BF), X, m).astype(F32)
    input_grad = (inv_all[:tok] * total).astype(BF)

    for axis, bit in (("c", 1), ("xl", 1), ("xh", 1), ("y", 1), ("y", 2), ("z", 1), ("z", 2), ("z", 4)):
        gsum = gsum + flip(gsum, axis, bit)
    gsum = lax.dynamic_slice_in_dim(gsum, (xl * 2 + c) * feat, feat, 1)[0]
    gain_grad = gsum / norm_gain.astype(F32) * scale
    return (gate_act, input_grad, weight_grad, gain_grad)


def solution(mesh):
    inner_mesh = Mesh(mesh.devices.reshape(SIZES), AXES)
    tokens, features = ("z", "y", "xh"), ("xl", "c")
    return jax.shard_map(
        body,
        mesh=inner_mesh,
        in_specs=(P(tokens, features), P(features), P(tokens, features), P(tokens, features)),
        out_specs=(P(tokens, features), P(tokens, features), P(tokens, features), P(features)),
        check_vma=False,
    )
```

```python
import jax
import jax.numpy as jnp
from jax import lax
from jax.experimental import pallas as pl
from jax.experimental.pallas import tpu as pltpu
from jax.sharding import Mesh, PartitionSpec as P

D = 2560
EPS = 1e-05
AXES = ("z", "y", "xh", "xl", "c")
SIZES = (8, 4, 2, 2, 2)
NUM = dict(zip(AXES, SIZES))
X = ("xh", "xl")
EXTRA = 16
BF = jnp.bfloat16
F32 = jnp.float32
VMEM_LIMIT = 48 * 1024 * 1024
NT = (((1,), (1,)), ((), ()))
TN = (((0,), (0,)), ((), ()))


def flip(a, axis, bit):
    names = axis if isinstance(axis, tuple) else (axis,)
    n = 1
    for name in names:
        n *= NUM[name]
    return lax.ppermute(a, axis, [(i, i ^ bit) for i in range(n)])


def after(value, *others):
    return lax.optimization_barrier((value,) + others)[0]


def pair(index, mine, other, axis):
    first = index == 0
    return jnp.concatenate([jnp.where(first, mine, other), jnp.where(first, other, mine)], axis=axis)


def ordered(p, index):
    low, high = (index % 2) == 0, (index // 2) == 0
    p = [jnp.where(low, p[k], p[k ^ 1]) for k in range(4)]
    return [jnp.where(high, p[k], p[k ^ 2]) for k in range(4)]


def rows_at(a, block, size):
    return lax.dynamic_slice_in_dim(a, block * size, size, 0)


def norm_kernel(place, mine, other, normed, inv_ref, gain_ref):
    xl, c = place[0], place[1]
    tok = normed.shape[0]
    feat = mine.shape[-1]
    total = jnp.zeros((tok, 1), F32)
    for src in (mine, other):
        for dxl in (0, 1):
            v = src[0, dxl, :tok, :].astype(F32)
            total = total + jnp.sum(v * v, axis=1, keepdims=True)
    inv = lax.rsqrt(total / D + EPS)
    inv_ref[...] = inv
    for dc, src in enumerate((mine, other)):
        for dxl in (0, 1):
            at = pl.multiple_of(((xl ^ dxl) * 2 + (c ^ dc)) * feat, 128)
            gain = src[0, dxl, tok:, :].astype(F32)[:1]
            v = src[0, dxl, :tok, :].astype(F32)
            normed[:, pl.ds(at, feat)] = (v * inv * gain).astype(BF)
            gain_ref[:, pl.ds(at, feat)] = gain


def norm_call(place, mine, other):
    groups, _, rows, feat = mine.shape
    tok = rows - EXTRA
    block = pl.BlockSpec((1, 2, rows, feat), lambda i, s: (i, 0, 0, 0))
    return pl.pallas_call(
        norm_kernel,
        out_shape=(
            jax.ShapeDtypeStruct((groups * tok, D), BF),
            jax.ShapeDtypeStruct((groups * tok, 1), F32),
            jax.ShapeDtypeStruct((1, D), F32),
        ),
        grid_spec=pltpu.PrefetchScalarGridSpec(
            num_scalar_prefetch=1,
            grid=(groups,),
            in_specs=[block, block],
            out_specs=(
                pl.BlockSpec((tok, D), lambda i, s: (i, 0)),
                pl.BlockSpec((tok, 1), lambda i, s: (i, 0)),
                pl.BlockSpec((1, D), lambda i, s: (0, 0)),
            ),
        ),
        compiler_params=pltpu.CompilerParams(vmem_limit_bytes=VMEM_LIMIT),
        cost_estimate=pl.CostEstimate(flops=8 * tok * D, bytes_accessed=8 * tok * D, transcendentals=0),
        name="norm",
    )(place, mine, other)


def gate_kernel(normed, weight, cot, act_ref, grad_ref, inner_ref):
    pre = jnp.dot(normed[...], weight[...], preferred_element_type=F32)
    sig = 1.0 / (1.0 + jnp.exp(-pre))
    act_ref[0] = (pre * sig).astype(BF)
    grad = (cot[0].astype(F32) * sig * (1.0 + pre * (1.0 - sig))).astype(BF)
    grad_ref[...] = grad
    inner_ref[...] = jnp.sum(grad.astype(F32) * pre, axis=1, keepdims=True) / D


def gate_call(normed, weight, cot):
    n, tok, hid = cot.shape
    slab = pl.BlockSpec((1, tok, hid), lambda i: (i, 0, 0))
    return pl.pallas_call(
        gate_kernel,
        out_shape=(
            jax.ShapeDtypeStruct((n, tok, hid), BF),
            jax.ShapeDtypeStruct((n * tok, hid), BF),
            jax.ShapeDtypeStruct((n * tok, 1), F32),
        ),
        grid=(n,),
        in_specs=[
            pl.BlockSpec((tok, D), lambda i: (i, 0)),
            pl.BlockSpec((D, hid), lambda i: (0, 0)),
            slab,
        ],
        out_specs=(
            slab,
            pl.BlockSpec((tok, hid), lambda i: (i, 0)),
            pl.BlockSpec((tok, 1), lambda i: (i, 0)),
        ),
        compiler_params=pltpu.CompilerParams(vmem_limit_bytes=VMEM_LIMIT),
        cost_estimate=pl.CostEstimate(
            flops=2 * n * tok * D * hid, bytes_accessed=2 * D * (n * tok + hid), transcendentals=n * tok * hid
        ),
        name="gate",
    )(normed, weight, cot)


def back_kernel(place, grad, weight, normed, inner, gain, out_ref):
    part = lax.dot_general(grad[...], weight[...], NT, preferred_element_type=F32)
    rows = normed[...].astype(F32)
    g = gain[...]
    out = (part * g - rows * inner[...] * (1.0 / g)).astype(BF)
    terms = jnp.sum(part * rows, axis=0, keepdims=True).astype(BF)
    terms = jnp.broadcast_to(terms, (EXTRA, terms.shape[1]))
    groups, rows_out, _ = out_ref.shape
    tok = rows_out - EXTRA
    for i in range(groups):
        out_ref[i, :tok, :] = out[i * tok:(i + 1) * tok]
        out_ref[i, tok:, :] = terms


def back_call(place, grad, weight, normed, inner, gain, dc, groups, feat):
    rows, hid = grad.shape
    tok = rows // groups
    which = lambda i, s: (s[0] ^ i) * 2 + (s[1] ^ dc)
    whole = lambda *shape: pl.BlockSpec(shape, lambda i, s: (0, 0))
    return pl.pallas_call(
        back_kernel,
        out_shape=jax.ShapeDtypeStruct((groups, tok + EXTRA, 2 * feat), BF),
        grid_spec=pltpu.PrefetchScalarGridSpec(
            num_scalar_prefetch=1,
            grid=(2,),
            in_specs=[
                whole(rows, hid),
                pl.BlockSpec((feat, hid), lambda i, s: (which(i, s), 0)),
                pl.BlockSpec((rows, feat), lambda i, s: (0, which(i, s))),
                whole(rows, 1),
                pl.BlockSpec((1, feat), lambda i, s: (0, which(i, s))),
            ],
            out_specs=pl.BlockSpec((groups, tok + EXTRA, feat), lambda i, s: (0, 0, i)),
        ),
        compiler_params=pltpu.CompilerParams(vmem_limit_bytes=VMEM_LIMIT),
        cost_estimate=pl.CostEstimate(
            flops=2 * rows * D * hid // 2, bytes_accessed=D * (3 * rows + hid), transcendentals=0
        ),
        name="back",
    )(place, grad, weight, normed, inner, gain)


def body(stream, norm_gain, gate_weight, act_grad):
    z, y, xh, xl, c = (lax.axis_index(a) for a in AXES)
    tok, feat = stream.shape
    hid = act_grad.shape[1] // 2
    wrows = gate_weight.shape[0]
    place = jnp.stack([xl, c]).astype(jnp.int32)
    scale = float(tok * 64) ** (-0.5)

    cut = lambda a, i: lax.dynamic_slice_in_dim(a, i * hid, hid, 1)
    w = pair(xh, cut(gate_weight, xh), flip(cut(gate_weight, 1 - xh), "xh", 1), 0)
    w = jnp.concatenate(ordered([w] + [flip(w, "y", k) for k in (1, 2, 3)], y), axis=0)
    weight = lax.all_gather(w, "z", axis=0, tiled=True)

    payload = jnp.concatenate([stream, jnp.broadcast_to(norm_gain[None], (EXTRA, feat))], axis=0)
    near = jnp.stack([payload] + [flip(payload, X, m) for m in (1, 2, 3)])
    near = near.reshape(2, 2, tok + EXTRA, feat)
    normed, inv_all, gain = norm_call(place, near, flip(near, "c", 1))

    cot = jnp.stack([cut(act_grad, xh), flip(cut(act_grad, 1 - xh), "xh", 1)])
    act, grad, inner = gate_call(normed, weight, cot)

    terms = lax.dot_general(normed, grad, TN, preferred_element_type=F32).astype(BF)
    sums_z = lax.psum_scatter(terms, "z", scatter_dimension=0, tiled=True)

    late = after(grad, terms)
    back = lambda dc: back_call(place, late, weight, normed, inner, gain, dc, 2, feat)
    first, second = back(1), back(0)
    sums = second.astype(F32) + flip(first, "c", 1).astype(F32)
    piece = lambda m: sums[m // 2, :, (m % 2) * feat:(m % 2 + 1) * feat].astype(BF)
    p = [piece(0).astype(F32)] + [flip(piece(m), X, m).astype(F32) for m in (1, 2, 3)]
    total = (p[0] + p[1]) + (p[2] + p[3])
    input_grad = (inv_all[:tok] * total[:tok]).astype(BF)

    act = after(act, second)
    gate_act = pair(xh, act[0], flip(act[1], "xh", 1), 1)

    gsum = total[tok:tok + 1]
    for axis, bit in (("z", 1), ("z", 2), ("z", 4), ("y", 1), ("y", 2)):
        gsum = gsum + flip(gsum, axis, bit)
    gain_grad = gsum[0] / norm_gain.astype(F32) * scale

    whole = rows_at(sums_z, y, 2 * wrows).astype(F32)
    for k in (1, 2, 3):
        whole = whole + flip(rows_at(sums_z, y ^ k, 2 * wrows), "y", k).astype(F32)
    other = flip(rows_at(whole, 1 - xh, wrows).astype(BF), "xh", 1).astype(F32)
    weight_grad = pair(xh, rows_at(whole, xh, wrows), other, 1) * scale
    return (gate_act, input_grad, weight_grad, gain_grad)


def solution(mesh):
    inner_mesh = Mesh(mesh.devices.reshape(SIZES), AXES)
    tokens, features = ("z", "y", "xh"), ("xl", "c")
    return jax.shard_map(
        body,
        mesh=inner_mesh,
        in_specs=(P(tokens, features), P(features), P(tokens, features), P(tokens, features)),
        out_specs=(P(tokens, features), P(tokens, features), P(tokens, features), P(features)),
        check_vma=False,
    )
```

```python
import jax
import jax.numpy as jnp
from jax import lax
from jax.experimental import pallas as pl
from jax.experimental.pallas import tpu as pltpu
from jax.sharding import Mesh, PartitionSpec as P

D = 2560
EPS = 1e-05
AXES = ("z", "y", "xh", "xl", "c")
SIZES = (8, 4, 2, 2, 2)
NUM = dict(zip(AXES, SIZES))
X = ("xh", "xl")
PART_A = 384
EXTRA = 16
BF = jnp.bfloat16
F32 = jnp.float32
VMEM_LIMIT = 32 * 1024 * 1024
NT = (((1,), (1,)), ((), ()))
TN = (((0,), (0,)), ((), ()))


def flip(a, axis, bit):
    names = axis if isinstance(axis, tuple) else (axis,)
    n = 1
    for name in names:
        n *= NUM[name]
    return lax.ppermute(a, axis, [(i, i ^ bit) for i in range(n)])


def together(*values):
    return lax.optimization_barrier(values)


def ring(a, d):
    n = NUM["z"]
    return lax.ppermute(a, "z", [(i, (i + d) % n) for i in range(n)])


def pair(index, mine, other, axis):
    first = index == 0
    return jnp.concatenate([jnp.where(first, mine, other), jnp.where(first, other, mine)], axis=axis)


def ordered(p, index):
    low, high = (index % 2) == 0, (index // 2) == 0
    p = [jnp.where(low, p[k], p[k ^ 1]) for k in range(4)]
    return [jnp.where(high, p[k], p[k ^ 2]) for k in range(4)]


def rows_at(a, block, size):
    return lax.dynamic_slice_in_dim(a, block * size, size, 0)


def norm_kernel(place, mine, other, normed, inv_ref, gain_ref):
    xl, c = place[0], place[1]
    tok = normed.shape[0]
    feat = mine.shape[-1]
    total = jnp.zeros((tok, 1), F32)
    for src in (mine, other):
        for dxl in (0, 1):
            v = src[0, dxl, :tok, :].astype(F32)
            total = total + jnp.sum(v * v, axis=1, keepdims=True)
    inv = lax.rsqrt(total / D + EPS)
    inv_ref[...] = inv
    for dc, src in enumerate((mine, other)):
        for dxl in (0, 1):
            at = pl.multiple_of(((xl ^ dxl) * 2 + (c ^ dc)) * feat, 128)
            gain = src[0, dxl, tok:, :].astype(F32)[:1]
            v = src[0, dxl, :tok, :].astype(F32)
            normed[:, pl.ds(at, feat)] = (v * inv * gain).astype(BF)
            gain_ref[:, pl.ds(at, feat)] = gain


def norm_call(place, mine, other):
    groups, _, rows, feat = mine.shape
    tok = rows - EXTRA
    block = pl.BlockSpec((1, 2, rows, feat), lambda i, s: (i, 0, 0, 0))
    return pl.pallas_call(
        norm_kernel,
        out_shape=(
            jax.ShapeDtypeStruct((groups * tok, D), BF),
            jax.ShapeDtypeStruct((groups * tok, 1), F32),
            jax.ShapeDtypeStruct((1, D), F32),
        ),
        grid_spec=pltpu.PrefetchScalarGridSpec(
            num_scalar_prefetch=1,
            grid=(groups,),
            in_specs=[block, block],
            out_specs=(
                pl.BlockSpec((tok, D), lambda i, s: (i, 0)),
                pl.BlockSpec((tok, 1), lambda i, s: (i, 0)),
                pl.BlockSpec((1, D), lambda i, s: (0, 0)),
            ),
        ),
        compiler_params=pltpu.CompilerParams(vmem_limit_bytes=VMEM_LIMIT),
        cost_estimate=pl.CostEstimate(flops=8 * tok * D, bytes_accessed=8 * tok * D, transcendentals=0),
        name="norm",
    )(place, mine, other)


def gate_kernel(start, normed, weight, cot, *refs):
    hid = weight.shape[1]
    pre = jnp.dot(normed[...], weight[...], preferred_element_type=F32)
    sig = 1.0 / (1.0 + jnp.exp(-pre))
    act = (pre * sig).astype(BF)
    grad = (cot[0, :, start:start + hid].astype(F32) * sig * (1.0 + pre * (1.0 - sig))).astype(BF)
    inner = jnp.sum(grad.astype(F32) * pre, axis=1, keepdims=True) / D
    if start:
        act_a, grad_a, inner_a = refs[:3]
        refs[3][0, :, :start] = act_a[0]
        refs[4][:, :start] = grad_a[...]
        inner = inner + inner_a[...]
    act_ref, grad_ref, inner_ref = refs[-3:]
    act_ref[0, :, start:start + hid] = act
    grad_ref[:, start:start + hid] = grad
    inner_ref[...] = inner


def gate_call(normed, weight, cot, start, *earlier):
    n, tok, width = cot.shape
    hid = weight.shape[1]
    col = pl.BlockSpec((tok, 1), lambda i: (i, 0))
    slab = lambda w: pl.BlockSpec((1, tok, w), lambda i: (i, 0, 0))
    rows = lambda w: pl.BlockSpec((tok, w), lambda i: (i, 0))
    return pl.pallas_call(
        lambda *refs: gate_kernel(start, *refs),
        out_shape=(
            jax.ShapeDtypeStruct((n, tok, start + hid), BF),
            jax.ShapeDtypeStruct((n * tok, start + hid), BF),
            jax.ShapeDtypeStruct((n * tok, 1), F32),
        ),
        grid=(n,),
        in_specs=[
            rows(D),
            pl.BlockSpec((D, hid), lambda i: (0, 0)),
            slab(width),
        ] + ([slab(start), rows(start), col] if start else []),
        out_specs=(slab(start + hid), rows(start + hid), col),
        compiler_params=pltpu.CompilerParams(vmem_limit_bytes=VMEM_LIMIT),
        cost_estimate=pl.CostEstimate(
            flops=2 * n * tok * D * hid, bytes_accessed=2 * D * (n * tok + hid), transcendentals=n * tok * hid
        ),
        name="gate",
    )(normed, weight, cot, *earlier)


def back_kernel(place, grad, weight_a, weight_b, normed, inner, gain, out_ref):
    part_a = weight_a.shape[1]
    part = lax.dot_general(grad[:, :part_a], weight_a[...], NT, preferred_element_type=F32)
    part = part + lax.dot_general(grad[:, part_a:], weight_b[...], NT, preferred_element_type=F32)
    rows = normed[...].astype(F32)
    g = gain[...]
    out = (part * g - rows * inner[...] * (1.0 / g)).astype(BF)
    terms = jnp.sum(part * rows, axis=0, keepdims=True).astype(BF)
    terms = jnp.broadcast_to(terms, (EXTRA, terms.shape[1]))
    groups, rows_out, _ = out_ref.shape
    tok = rows_out - EXTRA
    for i in range(groups):
        out_ref[i, :tok, :] = out[i * tok:(i + 1) * tok]
        out_ref[i, tok:, :] = terms


def back_call(place, grad, weight_a, weight_b, normed, inner, gain, dc, groups, feat):
    rows = grad.shape[0]
    tok = rows // groups
    which = lambda i, s: (s[0] ^ i) * 2 + (s[1] ^ dc)
    hid_a, hid_b = weight_a.shape[1], weight_b.shape[1]
    whole = lambda *shape: pl.BlockSpec(shape, lambda i, s: (0, 0))
    return pl.pallas_call(
        back_kernel,
        out_shape=jax.ShapeDtypeStruct((groups, tok + EXTRA, 2 * feat), BF),
        grid_spec=pltpu.PrefetchScalarGridSpec(
            num_scalar_prefetch=1,
            grid=(2,),
            in_specs=[
                whole(rows, hid_a + hid_b),
                pl.BlockSpec((feat, hid_a), lambda i, s: (which(i, s), 0)),
                pl.BlockSpec((feat, hid_b), lambda i, s: (which(i, s), 0)),
                pl.BlockSpec((rows, feat), lambda i, s: (0, which(i, s))),
                whole(rows, 1),
                pl.BlockSpec((1, feat), lambda i, s: (0, which(i, s))),
            ],
            out_specs=pl.BlockSpec((groups, tok + EXTRA, feat), lambda i, s: (0, 0, i)),
        ),
        compiler_params=pltpu.CompilerParams(vmem_limit_bytes=VMEM_LIMIT),
        cost_estimate=pl.CostEstimate(
            flops=2 * rows * D * (hid_a + hid_b) // 2, bytes_accessed=D * (3 * rows + hid_a + hid_b), transcendentals=0
        ),
        name="back",
    )(place, grad, weight_a, weight_b, normed, inner, gain)


def body(stream, norm_gain, gate_weight, act_grad):
    z, y, xh, xl, c = (lax.axis_index(a) for a in AXES)
    tok, feat = stream.shape
    hid = act_grad.shape[1] // 2
    wrows = gate_weight.shape[0]
    place = jnp.stack([xl, c]).astype(jnp.int32)
    scale = float(tok * 64) ** (-0.5)

    cut = lambda a, i: lax.dynamic_slice_in_dim(a, i * hid, hid, 1)
    w = pair(xh, cut(gate_weight, xh), flip(cut(gate_weight, 1 - xh), "xh", 1), 0)
    w_b = [w[:, PART_A:]]
    w_b = w_b + [flip(w_b[0], "y", k) for k in (1, 2, 3)]
    w_a = w[None, None, None, :, :PART_A]
    w_a = pair(z // 4, w_a, flip(w_a, "z", 4), 0)
    *w_b, stream = together(*w_b, stream)
    w_b = jnp.concatenate(ordered(w_b, y), axis=0)
    held = jnp.zeros((NUM["z"], *w_b.shape), BF)
    put = lambda held, block, i: lax.dynamic_update_index_in_dim(held, block, lax.rem(z + i, NUM["z"]), 0)
    held = put(held, w_b, 0)
    up = down = w_b
    for step in (1, 2, 3):
        up, down = ring(up, 1), ring(down, -1)
        if step == 1:
            up, down, act_grad = together(up, down, act_grad)
        held = put(put(held, up, NUM["z"] - step), down, step)
        if step < 3:
            w_a = pair((z // (4 >> step)) % 2, w_a, flip(w_a, "z", 4 >> step), step)
    last = ring(up, 1)
    weight_b = put(held, last, 4).reshape(D, hid - PART_A)
    w_a = w_a.reshape(NUM["z"], 2 * wrows, PART_A)

    payload = jnp.concatenate([stream, jnp.broadcast_to(norm_gain[None], (EXTRA, feat))], axis=0)
    near = jnp.stack([payload] + [flip(payload, X, m) for m in (1, 2, 3)])
    near = near.reshape(2, 2, tok + EXTRA, feat)
    normed, inv_all, gain = norm_call(place, near, flip(near, "c", 1))

    cot = jnp.stack([cut(act_grad, xh), flip(cut(act_grad, 1 - xh), "xh", 1)])

    w_a = [w_a] + [flip(w_a, "y", k) for k in (1, 2, 3)]
    *w_a, normed, cot = together(*w_a, normed, cot)
    weight_a = jnp.stack(ordered(w_a, y), axis=1).reshape(D, PART_A)

    act, grad, inner = gate_call(normed, weight_b, cot, PART_A, *gate_call(normed, weight_a, cot, 0))
    terms = lax.dot_general(normed, grad, TN, preferred_element_type=F32).astype(BF)
    terms, grad = together(terms, grad)
    sums_z = lax.psum_scatter(terms, "z", scatter_dimension=0, tiled=True)

    back = lambda dc: back_call(place, grad, weight_a, weight_b, normed, inner, gain, dc, 2, feat)
    first, second = back(1), back(0)
    sums = second.astype(F32) + flip(first, "c", 1).astype(F32)
    piece = lambda m: sums[m // 2, :, (m % 2) * feat:(m % 2 + 1) * feat].astype(BF)
    p = [piece(0).astype(F32)] + [flip(piece(m), X, m).astype(F32) for m in (1, 2, 3)]
    total = (p[0] + p[1]) + (p[2] + p[3])

    act, total = together(act, total)
    input_grad = (inv_all[:tok] * total[:tok]).astype(BF)
    gate_act = pair(xh, act[0], flip(act[1], "xh", 1), 1)

    gsum = sums[0, tok:tok + 1]
    for axis, bit in (("z", 1), ("z", 2), ("z", 4), ("y", 1), ("y", 2), ("xh", 1)):
        gsum = gsum + flip(gsum, axis, bit)
    gsum = gsum[:, :feat] + flip(gsum[:, feat:], "xl", 1)
    gain_grad = gsum[0] / norm_gain.astype(F32) * scale

    whole = rows_at(sums_z, y, 2 * wrows).astype(F32)
    for k in (1, 2, 3):
        whole = whole + flip(rows_at(sums_z, y ^ k, 2 * wrows), "y", k).astype(F32)
    other = flip(rows_at(whole, 1 - xh, wrows).astype(BF), "xh", 1).astype(F32)
    weight_grad = pair(xh, rows_at(whole, xh, wrows), other, 1) * scale
    return (gate_act, input_grad, weight_grad, gain_grad)


def solution(mesh):
    inner_mesh = Mesh(mesh.devices.reshape(SIZES), AXES)
    tokens, features = ("z", "y", "xh"), ("xl", "c")
    return jax.shard_map(
        body,
        mesh=inner_mesh,
        in_specs=(P(tokens, features), P(features), P(tokens, features), P(tokens, features)),
        out_specs=(P(tokens, features), P(tokens, features), P(tokens, features), P(features)),
        check_vma=False,
    )
```

```python
import jax
import jax.numpy as jnp
from jax import lax
from jax.experimental import pallas as pl
from jax.experimental.pallas import tpu as pltpu
from jax.sharding import Mesh, PartitionSpec as P

D = 2560
EPS = 1e-05
AXES = ("z", "y", "xh", "xl", "c")
SIZES = (8, 4, 2, 2, 2)
NUM = dict(zip(AXES, SIZES))
X = ("xh", "xl")
PART_A = 384
EXTRA = 16
BF = jnp.bfloat16
F32 = jnp.float32
VMEM_LIMIT = 32 * 1024 * 1024
NT = (((1,), (1,)), ((), ()))
TN = (((0,), (0,)), ((), ()))


def flip(a, axis, bit):
    names = axis if isinstance(axis, tuple) else (axis,)
    n = 1
    for name in names:
        n *= NUM[name]
    return lax.ppermute(a, axis, [(i, i ^ bit) for i in range(n)])


def together(*values):
    return lax.optimization_barrier(values)


def ring(a, d):
    n = NUM["z"]
    return lax.ppermute(a, "z", [(i, (i + d) % n) for i in range(n)])


def pair(index, mine, other, axis):
    first = index == 0
    return jnp.concatenate([jnp.where(first, mine, other), jnp.where(first, other, mine)], axis=axis)


def ordered(p, index):
    low, high = (index % 2) == 0, (index // 2) == 0
    p = [jnp.where(low, p[k], p[k ^ 1]) for k in range(4)]
    return [jnp.where(high, p[k], p[k ^ 2]) for k in range(4)]


def rows_at(a, block, size):
    return lax.dynamic_slice_in_dim(a, block * size, size, 0)


def norm_kernel(place, mine, other, normed, inv_ref, gain_ref):
    xl, c = place[0], place[1]
    tok = normed.shape[0]
    feat = mine.shape[-1]
    total = jnp.zeros((tok, 1), F32)
    for src in (mine, other):
        for dxl in (0, 1):
            v = src[0, dxl, :tok, :].astype(F32)
            total = total + jnp.sum(v * v, axis=1, keepdims=True)
    inv = lax.rsqrt(total / D + EPS)
    inv_ref[...] = inv
    for dc, src in enumerate((mine, other)):
        for dxl in (0, 1):
            at = pl.multiple_of(((xl ^ dxl) * 2 + (c ^ dc)) * feat, 128)
            gain = src[0, dxl, tok:, :].astype(F32)[:1]
            v = src[0, dxl, :tok, :].astype(F32)
            normed[:, pl.ds(at, feat)] = (v * inv * gain).astype(BF)
            gain_ref[:, pl.ds(at, feat)] = gain


def norm_call(place, mine, other):
    groups, _, rows, feat = mine.shape
    tok = rows - EXTRA
    block = pl.BlockSpec((1, 2, rows, feat), lambda i, s: (i, 0, 0, 0))
    return pl.pallas_call(
        norm_kernel,
        out_shape=(
            jax.ShapeDtypeStruct((groups * tok, D), BF),
            jax.ShapeDtypeStruct((groups * tok, 1), F32),
            jax.ShapeDtypeStruct((1, D), F32),
        ),
        grid_spec=pltpu.PrefetchScalarGridSpec(
            num_scalar_prefetch=1,
            grid=(groups,),
            in_specs=[block, block],
            out_specs=(
                pl.BlockSpec((tok, D), lambda i, s: (i, 0)),
                pl.BlockSpec((tok, 1), lambda i, s: (i, 0)),
                pl.BlockSpec((1, D), lambda i, s: (0, 0)),
            ),
        ),
        compiler_params=pltpu.CompilerParams(vmem_limit_bytes=VMEM_LIMIT),
        cost_estimate=pl.CostEstimate(flops=8 * tok * D, bytes_accessed=8 * tok * D, transcendentals=0),
        name="norm",
    )(place, mine, other)


def gate_kernel(start, normed, weight, cot, *refs):
    hid = weight.shape[1]
    pre = jnp.dot(normed[...], weight[...], preferred_element_type=F32)
    sig = 1.0 / (1.0 + jnp.exp(-pre))
    act = (pre * sig).astype(BF)
    grad = (cot[0, :, start:start + hid].astype(F32) * sig * (1.0 + pre * (1.0 - sig))).astype(BF)
    inner = jnp.sum(grad.astype(F32) * pre, axis=1, keepdims=True) / D
    if start:
        act_a, grad_a, inner_a = refs[:3]
        refs[3][0, :, :start] = act_a[0]
        refs[4][:, :start] = grad_a[...]
        inner = inner + inner_a[...]
    act_ref, grad_ref, inner_ref = refs[-3:]
    act_ref[0, :, start:start + hid] = act
    grad_ref[:, start:start + hid] = grad
    inner_ref[...] = inner


def gate_call(normed, weight, cot, start, *earlier):
    n, tok, width = cot.shape
    hid = weight.shape[1]
    col = pl.BlockSpec((tok, 1), lambda i: (i, 0))
    slab = lambda w: pl.BlockSpec((1, tok, w), lambda i: (i, 0, 0))
    rows = lambda w: pl.BlockSpec((tok, w), lambda i: (i, 0))
    return pl.pallas_call(
        lambda *refs: gate_kernel(start, *refs),
        out_shape=(
            jax.ShapeDtypeStruct((n, tok, start + hid), BF),
            jax.ShapeDtypeStruct((n * tok, start + hid), BF),
            jax.ShapeDtypeStruct((n * tok, 1), F32),
        ),
        grid=(n,),
        in_specs=[
            rows(D),
            pl.BlockSpec((D, hid), lambda i: (0, 0)),
            slab(width),
        ] + ([slab(start), rows(start), col] if start else []),
        out_specs=(slab(start + hid), rows(start + hid), col),
        compiler_params=pltpu.CompilerParams(vmem_limit_bytes=VMEM_LIMIT),
        cost_estimate=pl.CostEstimate(
            flops=2 * n * tok * D * hid, bytes_accessed=2 * D * (n * tok + hid), transcendentals=n * tok * hid
        ),
        name="gate",
    )(normed, weight, cot, *earlier)


def back_kernel(place, grad, weight_a, weight_b, normed, inner, gain, out_ref):
    part_a = weight_a.shape[1]
    part = lax.dot_general(grad[:, :part_a], weight_a[...], NT, preferred_element_type=F32)
    part = part + lax.dot_general(grad[:, part_a:], weight_b[...], NT, preferred_element_type=F32)
    rows = normed[...].astype(F32)
    g = gain[...]
    out = (part * g - rows * inner[...] * (1.0 / g)).astype(BF)
    terms = jnp.sum(part * rows, axis=0, keepdims=True).astype(BF)
    terms = jnp.broadcast_to(terms, (EXTRA, terms.shape[1]))
    groups, rows_out, _ = out_ref.shape
    tok = rows_out - EXTRA
    for i in range(groups):
        out_ref[i, :tok, :] = out[i * tok:(i + 1) * tok]
        out_ref[i, tok:, :] = terms


def back_call(place, grad, weight_a, weight_b, normed, inner, gain, dc, groups, feat):
    rows = grad.shape[0]
    tok = rows // groups
    which = lambda i, s: (s[0] ^ i) * 2 + (s[1] ^ dc)
    hid_a, hid_b = weight_a.shape[1], weight_b.shape[1]
    whole = lambda *shape: pl.BlockSpec(shape, lambda i, s: (0, 0))
    return pl.pallas_call(
        back_kernel,
        out_shape=jax.ShapeDtypeStruct((groups, tok + EXTRA, 2 * feat), BF),
        grid_spec=pltpu.PrefetchScalarGridSpec(
            num_scalar_prefetch=1,
            grid=(2,),
            in_specs=[
                whole(rows, hid_a + hid_b),
                pl.BlockSpec((feat, hid_a), lambda i, s: (which(i, s), 0)),
                pl.BlockSpec((feat, hid_b), lambda i, s: (which(i, s), 0)),
                pl.BlockSpec((rows, feat), lambda i, s: (0, which(i, s))),
                whole(rows, 1),
                pl.BlockSpec((1, feat), lambda i, s: (0, which(i, s))),
            ],
            out_specs=pl.BlockSpec((groups, tok + EXTRA, feat), lambda i, s: (0, 0, i)),
        ),
        compiler_params=pltpu.CompilerParams(vmem_limit_bytes=VMEM_LIMIT),
        cost_estimate=pl.CostEstimate(
            flops=2 * rows * D * (hid_a + hid_b) // 2, bytes_accessed=D * (3 * rows + hid_a + hid_b), transcendentals=0
        ),
        name="back",
    )(place, grad, weight_a, weight_b, normed, inner, gain)


def body(stream, norm_gain, gate_weight, act_grad):
    z, y, xh, xl, c = (lax.axis_index(a) for a in AXES)
    tok, feat = stream.shape
    hid = act_grad.shape[1] // 2
    wrows = gate_weight.shape[0]
    place = jnp.stack([xl, c]).astype(jnp.int32)
    scale = float(tok * 64) ** (-0.5)

    cut = lambda a, i: lax.dynamic_slice_in_dim(a, i * hid, hid, 1)
    w = pair(xh, cut(gate_weight, xh), flip(cut(gate_weight, 1 - xh), "xh", 1), 0)
    w_b = [w[:, PART_A:]]
    w_b = w_b + [flip(w_b[0], "y", k) for k in (1, 2, 3)]
    w_a = w[None, None, None, :, :PART_A]
    w_a = pair(z // 4, w_a, flip(w_a, "z", 4), 0)
    *w_b, stream, act_grad = together(*w_b, stream, act_grad)
    w_b = jnp.concatenate(ordered(w_b, y), axis=0)
    held = jnp.zeros((NUM["z"], *w_b.shape), BF)
    put = lambda held, block, i: lax.dynamic_update_index_in_dim(held, block, lax.rem(z + i, NUM["z"]), 0)
    held = put(held, w_b, 0)
    up = down = w_b
    for step in (1, 2, 3):
        up, down = ring(up, 1), ring(down, -1)
        held = put(put(held, up, NUM["z"] - step), down, step)
        if step < 3:
            w_a = pair((z // (4 >> step)) % 2, w_a, flip(w_a, "z", 4 >> step), step)
    last = ring(up, 1)
    weight_b = put(held, last, 4).reshape(D, hid - PART_A)
    w_a = w_a.reshape(NUM["z"], 2 * wrows, PART_A)

    payload = jnp.concatenate([stream, jnp.broadcast_to(norm_gain[None], (EXTRA, feat))], axis=0)
    near = jnp.stack([payload] + [flip(payload, X, m) for m in (1, 2, 3)])
    near = near.reshape(2, 2, tok + EXTRA, feat)
    normed, inv_all, gain = norm_call(place, near, flip(near, "c", 1))

    cot = jnp.stack([cut(act_grad, xh), flip(cut(act_grad, 1 - xh), "xh", 1)])

    w_a = [w_a] + [flip(w_a, "y", k) for k in (1, 2, 3)]
    *w_a, normed, cot = together(*w_a, normed, cot)
    weight_a = jnp.stack(ordered(w_a, y), axis=1).reshape(D, PART_A)

    act, grad, inner = gate_call(normed, weight_b, cot, PART_A, *gate_call(normed, weight_a, cot, 0))
    terms = lax.dot_general(normed, grad, TN, preferred_element_type=F32).astype(BF)
    terms, grad = together(terms, grad)
    sums_z = lax.psum_scatter(terms, "z", scatter_dimension=0, tiled=True)

    back = lambda dc: back_call(place, grad, weight_a, weight_b, normed, inner, gain, dc, 2, feat)
    first, second = back(1), back(0)
    sums = second.astype(F32) + flip(first, "c", 1).astype(F32)
    piece = lambda m: sums[m // 2, :, (m % 2) * feat:(m % 2 + 1) * feat].astype(BF)
    p = [piece(0).astype(F32)] + [flip(piece(m), X, m).astype(F32) for m in (1, 2, 3)]
    total = (p[0] + p[1]) + (p[2] + p[3])

    act, total = together(act, total)
    input_grad = (inv_all[:tok] * total[:tok]).astype(BF)
    gate_act = pair(xh, act[0], flip(act[1], "xh", 1), 1)

    gsum = sums[0, tok:tok + 1]
    for axis, bit in (("z", 1), ("z", 2), ("z", 4), ("y", 1), ("y", 2), ("xh", 1)):
        gsum = gsum + flip(gsum, axis, bit)
    gsum = gsum[:, :feat] + flip(gsum[:, feat:], "xl", 1)
    gain_grad = gsum[0] / norm_gain.astype(F32) * scale

    whole = rows_at(sums_z, y, 2 * wrows).astype(F32)
    for k in (1, 2, 3):
        whole = whole + flip(rows_at(sums_z, y ^ k, 2 * wrows), "y", k).astype(F32)
    other = flip(rows_at(whole, 1 - xh, wrows).astype(BF), "xh", 1).astype(F32)
    weight_grad = pair(xh, rows_at(whole, xh, wrows), other, 1) * scale
    return (gate_act, input_grad, weight_grad, gain_grad)


def solution(mesh):
    inner_mesh = Mesh(mesh.devices.reshape(SIZES), AXES)
    tokens, features = ("z", "y", "xh"), ("xl", "c")
    return jax.shard_map(
        body,
        mesh=inner_mesh,
        in_specs=(P(tokens, features), P(features), P(tokens, features), P(tokens, features)),
        out_specs=(P(tokens, features), P(tokens, features), P(tokens, features), P(features)),
        check_vma=False,
    )
```
